32 devices in a mesh: dp: 8 (over z, core), tensor: 4 (over y, x).
Axes of the slice: x: 2, y: 2, z: 4, core: 2. Of those that a mesh axis runs over, the one named last changes fastest.
Arguments:
- inputs: bfloat16 [6144, 8192], P(('dp', 'tensor')), may hold values from -70 to 70
- kv_grad: bfloat16 [6144, 2048], P('dp', 'tensor'), may hold values from -70 to 70
- master: float32 [8192, 2048], P('dp', 'tensor'), may hold values from -4 to 4
- first: float32 [8192, 2048], P('dp', 'tensor'), may hold values from -4 to 4
- second: float32 [8192, 2048], P('dp', 'tensor'), may hold values from 0.5 to 8
- clip_limit: float32 [1], replicated, may hold values from 8192 to 16384
Outputs:
- new_master: float32 [8192, 2048], P('dp', 'tensor')
- new_first: float32 [8192, 2048], P('dp', 'tensor')
- new_second: float32 [8192, 2048], P('dp', 'tensor')
The draws below stay inside these ranges and needn't reach their ends.
All inputs are finite; a program needn't handle non-finite values.
Results may differ from the reference program's by a relative error of at most 0.0003.
Values may be sent and summed in bfloat16 or wider, within the bound.
No kernel may reach another device: no remote copies, remote signals or barrier semaphores. Data moves between devices by JAX's collectives and lax.ppermute only.
A program may use at most 128 MiB of HBM per device.

```python
import math
import jax
import jax.numpy as jnp

D = 8192
STEP = 20
KV = 2048
TOKENS = 6144


def feature_scale(key, number, power):
    spread = jnp.exp(jax.random.uniform(key, (number,), jnp.float32) * math.log(10.0))
    position = jnp.arange(number, dtype=jnp.float32) / max(number - 1, 1)
    return spread * jnp.exp(position * (power * math.log(3.0)))


def token_factor(key):
    shared_key = jax.random.fold_in(key, 7)
    return jnp.clip(jax.random.normal(shared_key, (TOKENS,), jnp.float32), -4.0, 4.0)


def add_shared(values, factor, direction_key, columns, ceiling):
    direction = jnp.clip(jax.random.normal(direction_key, (columns,), jnp.float32), -4.0, 4.0)
    amplitude = float(TOKENS) ** (-0.25)
    mixed = values + amplitude * factor[:, None] * direction[None, :]
    return jnp.clip(mixed, -ceiling, ceiling)


def draw_inputs(key, part):
    factor = token_factor(key)
    key = jax.random.fold_in(key, 11)
    scale_key = jax.random.fold_in(key, 0)
    value_key = jax.random.fold_in(key, 1)
    direction_key = jax.random.fold_in(key, 3)
    values = jnp.clip(jax.random.normal(value_key, (TOKENS, D), jnp.float32), -4.0, 4.0)
    values = add_shared(values, factor, direction_key, D, 4.0)
    scale = feature_scale(scale_key, D, 0.5)
    return (values * scale[None, :]).astype(jnp.bfloat16)


def draw_kv_grad(key, part):
    factor = token_factor(key)
    key = jax.random.fold_in(key, 12)
    scale_key, value_key, direction_key = jax.random.split(key, 3)
    values = jnp.clip(jax.random.normal(value_key, (TOKENS, KV), jnp.float32), -4.0, 4.0)
    values = add_shared(values, factor, direction_key, KV, 4.0)
    scale = feature_scale(scale_key, KV, 0.5)
    return (values * scale[None, :]).astype(jnp.bfloat16)


def levels(key, extent, cuts, least, largest):
    level, own = 1.0, jax.random.fold_in(key, 6)
    for axis_at, blocks in cuts:
        steps = jnp.exp(jax.random.uniform(jax.random.fold_in(own, axis_at), (blocks,), jnp.float32, least / len(cuts), largest / len(cuts)))
        level = level * jnp.repeat(steps, extent[axis_at] // blocks).reshape([-1 if axis == axis_at else 1 for axis in range(len(extent))])
    return level


def gaussian(rng, dims, scale, bound, cuts=(), kind=jnp.bfloat16):
    loudness = levels(rng, dims, cuts, -0.22, 0.18) if cuts else 1.0
    result = jax.random.normal(rng, dims, jnp.float32) * scale * loudness
    return jnp.minimum(jnp.maximum(result, -bound), bound).astype(kind)


def setup_inputs(seed: int = 0) -> dict:
    splits = jax.random.split(jax.random.key(seed), 7)
    inputs = draw_inputs(jax.random.fold_in(splits[6], 71), 0)
    kv_grad = draw_kv_grad(jax.random.fold_in(splits[6], 71), 0)
    master = gaussian(splits[2], (D, KV), 1.0, 4.0, ((0, 8), (1, 4)), jnp.float32)
    first = gaussian(splits[3], (D, KV), 1.0, 4.0, ((0, 8), (1, 4)), jnp.float32)
    second = jnp.clip(jnp.exp(math.log(8.0) - 2.7725887 * jax.random.uniform(splits[4], (D, KV), jnp.float32) ** levels(splits[4], (D, KV), ((0, 8), (1, 4)), -0.2, 0.2)), 0.5, 8.0)
    clip_limit = jnp.clip(jnp.exp(jax.random.uniform(splits[5], (1,), jnp.float32, math.log(8192.0), math.log(16384.0))), 8192.0, 16384.0)
    return {"inputs": inputs, "kv_grad": kv_grad, "master": master, "first": first, "second": second, "clip_limit": clip_limit}


beta_first = 0.9
beta_second = 0.95
learn_rate = 0.00015
decay_rate = 0.1

def adam_update(gradient, square_sum, master, first, second, clip_limit):
    grad_norm = jnp.sqrt(square_sum)
    clip_factor = jnp.minimum(1.0, clip_limit[0] / (grad_norm + 1e-06))
    scaled = gradient * clip_factor
    new_first = beta_first * first + (1.0 - beta_first) * scaled
    new_second = beta_second * second + (1.0 - beta_second) * scaled * scaled
    first_hat = new_first / (1.0 - beta_first ** STEP)
    second_hat = new_second / (1.0 - beta_second ** STEP)
    new_master = master - learn_rate * (first_hat / (jnp.sqrt(second_hat) + 1e-08) + decay_rate * master)
    return (new_master, new_first, new_second)

def reference(inputs, kv_grad, master, first, second, clip_limit):
    gradient = jnp.dot(inputs.T, kv_grad, preferred_element_type=jnp.float32)
    square_sum = jnp.sum(gradient * gradient)
    new_master, new_first, new_second = adam_update(gradient, square_sum, master, first, second, clip_limit)
    return (new_master, new_first, new_second)
```

```python
import functools

import jax
import jax.numpy as jnp
from jax import lax
from jax.experimental import pallas as pl
from jax.experimental.pallas import tpu as pltpu
from jax.sharding import PartitionSpec as P

STEP = 20

beta_first = 0.9
beta_second = 0.95
learn_rate = 0.00015
decay_rate = 0.1

AXES = ("dp", "tensor")
SCALE_ROWS = 16
KNEE = 64.0
POWER = 32
SHIFT = 3.5
VMEM = 40 * 1024 * 1024


def encode(values, scale):
    u = jnp.abs(values) * (KNEE / jnp.maximum(scale, 1e-30))
    w = (u + jnp.sqrt(u * u + 1.0)) * (2.0**-SHIFT)
    power = 1
    while power < POWER:
        w = w * w
        power *= 2
    return jnp.where(values < 0, -w, w).astype(jnp.bfloat16)


def decode(code, scale):
    code = code.astype(jnp.float32)
    log_w = jnp.log(jnp.maximum(jnp.abs(code), 2.0 ** (-SHIFT * POWER))) * (1.0 / POWER) + SHIFT * 0.6931471805599453
    u = jnp.exp(log_w) - jnp.exp(-log_w)
    size = u * (scale * (0.5 / KNEE))
    return jnp.where(code < 0, -size, size)


def tile_rows(rows):
    return 128 if rows % 128 == 0 else rows


def product(a_refs, b_ref, columns):
    start, total = 0, None
    for a_ref in a_refs:
        depth = a_ref.shape[0]
        part = lax.dot_general(
            a_ref[:, columns],
            b_ref[pl.ds(start, depth), :],
            (((0,), (0,)), ((), ())),
            preferred_element_type=jnp.float32,
        )
        total = part if total is None else total + part
        start += depth
    return total


def chunk_kernel(n_a, n_in, mode, *refs):
    a_refs, b_ref, in_refs = refs[:n_a], refs[n_a], refs[n_a + 1 : n_a + 1 + n_in]
    rest = refs[n_a + 1 + n_in :]
    rows, width = a_refs[0].shape[1], b_ref.shape[1]
    tile = tile_rows(rows)

    def values(at):
        total = product(a_refs, b_ref, pl.ds(at, tile))
        for ref in in_refs:
            scale = ref[rows : rows + 1, :].astype(jnp.float32)
            total = total + decode(ref[pl.ds(at, tile), :], scale)
        return total

    if mode == "final":
        out_ref, square_ref = rest
        square = jnp.zeros((8, width), jnp.float32)
        for at in range(0, rows, tile):
            total = values(at)
            out_ref[pl.ds(at, tile), :] = total
            square = square + jnp.sum((total * total).reshape(tile // 8, 8, width), axis=0)
        square_ref[...] = sum(square[:, s : s + 128] for s in range(0, width, 128))
        return
    out_ref, held = rest
    largest = jnp.zeros((8, width), jnp.float32)
    for at in range(0, rows, tile):
        total = values(at)
        held[pl.ds(at, tile), :] = total
        largest = jnp.maximum(largest, jnp.max(jnp.abs(total).reshape(tile // 8, 8, width), axis=0))
    scale = jnp.max(largest, axis=0, keepdims=True).astype(jnp.bfloat16)
    out_ref[pl.ds(rows, SCALE_ROWS), :] = jnp.broadcast_to(scale, (SCALE_ROWS, width))
    scale = scale.astype(jnp.float32)
    for at in range(0, rows, tile):
        out_ref[pl.ds(at, tile), :] = encode(held[pl.ds(at, tile), :], scale)


def run_chunk(pieces, b, messages, mode):
    rows, width = pieces[0].shape[1], b.shape[1]
    if mode == "final":
        out_shape = (
            jax.ShapeDtypeStruct((rows, width), jnp.float32),
            jax.ShapeDtypeStruct((8, 128), jnp.float32),
        )
        scratch = []
    else:
        out_shape = jax.ShapeDtypeStruct((rows + SCALE_ROWS, width), jnp.bfloat16)
        scratch = [pltpu.VMEM((rows, width), jnp.float32)]
    depth = sum(p.shape[0] for p in pieces)
    cost = pl.CostEstimate(
        flops=2 * depth * rows * width,
        bytes_accessed=2 * depth * (rows + width) + 2 * rows * width * (len(messages) + 2),
        transcendentals=3 * rows * width * (len(messages) + 1),
    )
    return pl.pallas_call(
        functools.partial(chunk_kernel, len(pieces), len(messages), mode),
        out_shape=out_shape,
        scratch_shapes=scratch,
        cost_estimate=cost,
        compiler_params=pltpu.CompilerParams(vmem_limit_bytes=VMEM),
    )(*pieces, b, *messages)


def adam_update(gradient, square_sum, master, first, second, clip_limit):
    grad_norm = jnp.sqrt(square_sum)
    clip_factor = jnp.minimum(1.0, clip_limit[0] / (grad_norm + 1e-06))
    scaled = gradient * clip_factor
    new_first = beta_first * first + (1.0 - beta_first) * scaled
    new_second = beta_second * second + (1.0 - beta_second) * scaled * scaled
    first_hat = new_first / (1.0 - beta_first**STEP)
    second_hat = new_second / (1.0 - beta_second**STEP)
    new_master = master - learn_rate * (
        first_hat / (jnp.sqrt(second_hat) + 1e-08) + decay_rate * master
    )
    return (new_master, new_first, new_second)


def on_device(n_dp, n_tensor, inputs, kv_grad, master, first, second, clip_limit):
    n_z = n_dp // 2
    dp, me = lax.axis_index("dp"), lax.axis_index("tensor")
    z, core = dp // 2, dp % 2
    tokens, block = inputs.shape[0], master.shape[0]
    half = block // 2

    def send(x, move):
        pairs = []
        for g in range(n_dp):
            for t in range(n_tensor):
                to = move(g // 2, g % 2, t)
                if to is not None:
                    pairs.append((g * n_tensor + t, (to[0] * 2 + to[1]) * n_tensor + to[2]))
        return lax.ppermute(x, AXES, pairs)

    def over_core(x):
        return send(x, lambda z, c, t: (z, 1 - c, t))

    def over_tensor(x, bit):
        return send(x, lambda z, c, t: (z, c, t ^ bit))

    def over_z(x, bits):
        return send(x, lambda z, c, t: (z ^ bits, c, t))

    order = list(range(n_z - 1, -1, -1))

    def columns(k, owner_core, h):
        return ((z ^ k) * 2 + owner_core) * block + h * half

    def own_tokens(k, h):
        return lax.dynamic_slice(inputs, (0, columns(k, core, h)), (tokens, half))

    def for_other_core(k):
        return lax.dynamic_slice(inputs, (0, columns(k, 1 - core, 0)), (tokens, block))

    from_core = {}
    for k in order:
        from_core[k] = over_core(for_other_core(k))

    def chip_tokens(k, h):
        return jnp.concatenate([own_tokens(k, h), from_core[k][:, h * half : (h + 1) * half]], axis=0)

    bits = [1 << i for i in range((n_tensor - 1).bit_length())]
    ways = []
    for q in range(2):
        partner = bits[q]
        gather = [bit for bit in bits if bit != partner]
        at = [0]
        for bit in gather:
            at = at + [m ^ bit for m in at]
        ways.append((partner, gather, at))

    def rows_of(array, mine):
        return lax.dynamic_slice(array, (mine * tokens, 0), (tokens, array.shape[1]))

    kv_other = over_core(kv_grad)
    kv_mine, kv_theirs = [], []
    for partner, gather, at in ways:
        kv_mine.append(
            jnp.concatenate(
                [rows_of(array, me ^ m) for m in at for array in (kv_grad, kv_other)], axis=0
            )
        )
        mine = jnp.concatenate([rows_of(kv_grad, me ^ partner ^ m) for m in at], axis=0)
        got = over_tensor(mine, partner)
        other = over_core(got)
        kv_theirs.append(
            jnp.concatenate(
                [array[i * tokens : (i + 1) * tokens] for i in range(len(at)) for array in (got, other)],
                axis=0,
            )
        )

    chunks = [(k, h) for k in order for h in range(2)]
    arrived = {}
    for index, (k, h) in enumerate(chunks):
        partner, gather, at = ways[h]
        piece = chip_tokens(k, h)
        if index >= 2:
            before = chunks[index - 2]
            piece, arrived[before][-1] = lax.optimization_barrier((piece, arrived[before][-1]))
        pieces = [piece]
        for bit in gather:
            pieces = pieces + [over_tensor(p, bit) for p in pieces]
        arrived[(k, h)] = pieces

    to_merge, to_sum = {}, {0: [], 1: []}
    grads, squares = [], []
    for k, h in chunks:
        partner = ways[h][0]
        pieces = arrived[(k, h)]
        theirs = run_chunk(pieces, kv_theirs[h], [], "send")
        messages = [over_tensor(theirs, partner)]
        if k == 0:
            grad, square = run_chunk(pieces, kv_mine[h], messages + to_sum[h], "final")
            grads.append(grad)
            squares.append(square)
            continue
        if n_z == 4 and k == 2:
            messages.append(to_merge[h])
        summed = run_chunk(pieces, kv_mine[h], messages, "send")
        if n_z == 4 and k == 3:
            to_merge[h] = send(summed, lambda z, c, t: {0: (1, c, t), 3: (2, c, t)}.get(z))
            to_sum[h].append(send(summed, lambda z, c, t: {1: (2, c, t), 2: (1, c, t)}.get(z)))
        else:
            to_sum[h].append(over_z(summed, k))

    square = squares[0] + squares[1]
    square = square + over_core(square)
    square = square + sum(over_tensor(square, m) for m in range(1, n_tensor))
    square = square + sum(over_z(square, k) for k in range(1, n_z))
    square_sum = jnp.sum(square)
    gradient = jnp.concatenate(grads, axis=0)
    return adam_update(gradient, square_sum, master, first, second, clip_limit)


def solution(mesh):
    in_specs = (
        P(("dp", "tensor"), None),
        P("dp", "tensor"),
        P("dp", "tensor"),
        P("dp", "tensor"),
        P("dp", "tensor"),
        P(),
    )
    out_specs = (P("dp", "tensor"), P("dp", "tensor"), P("dp", "tensor"))
    return jax.shard_map(
        functools.partial(on_device, mesh.shape["dp"], mesh.shape["tensor"]),
        mesh=mesh,
        in_specs=in_specs,
        out_specs=out_specs,
        check_vma=False,
    )
```

```python
import functools

import jax
import jax.numpy as jnp
from jax import lax
from jax.experimental import pallas as pl
from jax.experimental.pallas import tpu as pltpu
from jax.sharding import PartitionSpec as P

STEP = 20

beta_first = 0.9
beta_second = 0.95
learn_rate = 0.00015
decay_rate = 0.1

AXES = ("dp", "tensor")
SCALE_ROWS = 16
KNEE = 64.0
POWER = 32
SHIFT = 3.5
VMEM = 40 * 1024 * 1024


def encode(values, scale):
    u = jnp.abs(values) * (KNEE / jnp.maximum(scale, 1e-30))
    w = (u + jnp.sqrt(u * u + 1.0)) * (2.0**-SHIFT)
    power = 1
    while power < POWER:
        w = w * w
        power *= 2
    return jnp.where(values < 0, -w, w).astype(jnp.bfloat16)


def decode(code, scale):
    code = code.astype(jnp.float32)
    log_w = jnp.log(jnp.maximum(jnp.abs(code), 2.0 ** (-SHIFT * POWER))) * (1.0 / POWER) + SHIFT * 0.6931471805599453
    u = jnp.exp(log_w) - jnp.exp(-log_w)
    size = u * (scale * (0.5 / KNEE))
    return jnp.where(code < 0, -size, size)


def tile_rows(rows):
    return 128 if rows % 128 == 0 else rows


def product(a_refs, b_ref, columns):
    start, total = 0, None
    for a_ref in a_refs:
        depth = a_ref.shape[0]
        part = lax.dot_general(
            a_ref[:, columns],
            b_ref[pl.ds(start, depth), :],
            (((0,), (0,)), ((), ())),
            preferred_element_type=jnp.float32,
        )
        total = part if total is None else total + part
        start += depth
    return total


def chunk_kernel(n_a, n_in, mode, *refs):
    a_refs, b_ref, in_refs = refs[:n_a], refs[n_a], refs[n_a + 1 : n_a + 1 + n_in]
    rest = refs[n_a + 1 + n_in :]
    rows, width = a_refs[0].shape[1], b_ref.shape[1]
    tile = tile_rows(rows)

    def values(at):
        total = product(a_refs, b_ref, pl.ds(at, tile))
        for ref in in_refs:
            scale = ref[rows : rows + 1, :].astype(jnp.float32)
            total = total + decode(ref[pl.ds(at, tile), :], scale)
        return total

    if mode == "final":
        out_ref, square_ref = rest
        square = jnp.zeros((8, width), jnp.float32)
        for at in range(0, rows, tile):
            total = values(at)
            out_ref[pl.ds(at, tile), :] = total
            square = square + jnp.sum((total * total).reshape(tile // 8, 8, width), axis=0)
        square_ref[...] = sum(square[:, s : s + 128] for s in range(0, width, 128))
        return
    out_ref, held = rest
    largest = jnp.zeros((8, width), jnp.float32)
    for at in range(0, rows, tile):
        total = values(at)
        held[pl.ds(at, tile), :] = total
        largest = jnp.maximum(largest, jnp.max(jnp.abs(total).reshape(tile // 8, 8, width), axis=0))
    scale = jnp.max(largest, axis=0, keepdims=True).astype(jnp.bfloat16)
    out_ref[pl.ds(rows, SCALE_ROWS), :] = jnp.broadcast_to(scale, (SCALE_ROWS, width))
    scale = scale.astype(jnp.float32)
    for at in range(0, rows, tile):
        out_ref[pl.ds(at, tile), :] = encode(held[pl.ds(at, tile), :], scale)


def run_chunk(pieces, b, messages, mode):
    rows, width = pieces[0].shape[1], b.shape[1]
    if mode == "final":
        out_shape = (
            jax.ShapeDtypeStruct((rows, width), jnp.float32),
            jax.ShapeDtypeStruct((8, 128), jnp.float32),
        )
        scratch = []
    else:
        out_shape = jax.ShapeDtypeStruct((rows + SCALE_ROWS, width), jnp.bfloat16)
        scratch = [pltpu.VMEM((rows, width), jnp.float32)]
    cost = pl.CostEstimate(flops=1024, bytes_accessed=1024, transcendentals=0)
    return pl.pallas_call(
        functools.partial(chunk_kernel, len(pieces), len(messages), mode),
        out_shape=out_shape,
        scratch_shapes=scratch,
        cost_estimate=cost,
        compiler_params=pltpu.CompilerParams(vmem_limit_bytes=VMEM),
    )(*pieces, b, *messages)


def adam_update(gradient, square_sum, master, first, second, clip_limit):
    grad_norm = jnp.sqrt(square_sum)
    clip_factor = jnp.minimum(1.0, clip_limit[0] / (grad_norm + 1e-06))
    scaled = gradient * clip_factor
    new_first = beta_first * first + (1.0 - beta_first) * scaled
    new_second = beta_second * second + (1.0 - beta_second) * scaled * scaled
    first_hat = new_first / (1.0 - beta_first**STEP)
    second_hat = new_second / (1.0 - beta_second**STEP)
    new_master = master - learn_rate * (
        first_hat / (jnp.sqrt(second_hat) + 1e-08) + decay_rate * master
    )
    return (new_master, new_first, new_second)


def on_device(n_dp, n_tensor, inputs, kv_grad, master, first, second, clip_limit):
    n_z = n_dp // 2
    dp, me = lax.axis_index("dp"), lax.axis_index("tensor")
    z, core = dp // 2, dp % 2
    tokens, block = inputs.shape[0], master.shape[0]
    half = block // 2

    def send(x, move):
        pairs = []
        for g in range(n_dp):
            for t in range(n_tensor):
                to = move(g // 2, g % 2, t)
                if to is not None:
                    pairs.append((g * n_tensor + t, (to[0] * 2 + to[1]) * n_tensor + to[2]))
        return lax.ppermute(x, AXES, pairs)

    def over_core(x):
        return send(x, lambda z, c, t: (z, 1 - c, t))

    def over_tensor(x, bit):
        return send(x, lambda z, c, t: (z, c, t ^ bit))

    def over_z(x, bits):
        return send(x, lambda z, c, t: (z ^ bits, c, t))

    def place_of(z):
        return jnp.where(z % 2 == 0, z // 2, n_z - (z + 1) // 2)

    def at_place(place):
        place = place % n_z
        return jnp.where(place < (n_z + 1) // 2, 2 * place, 2 * (n_z - place) - 1)

    ring = list(range(0, n_z, 2)) + list(range(n_z - 1 - n_z % 2, 0, -2))
    ways_round = (1, -1)

    def hand_on(x, h):
        return send(x, lambda z, c, t: (ring[(ring.index(z) + ways_round[h]) % n_z], c, t))

    def columns(s, owner_core, h):
        owner = at_place(place_of(z) - ways_round[h] * s)
        return (owner * 2 + owner_core) * block + h * half

    def own_tokens(s, h, owner_core):
        return lax.dynamic_slice(inputs, (0, columns(s, owner_core, h)), (tokens, half))

    steps = list(range(1, n_z + 1))
    from_core = {}
    for s in steps:
        mine = jnp.concatenate([own_tokens(s, h, 1 - core) for h in range(2)], axis=0)
        if s > 1:
            mine, from_core[1] = lax.optimization_barrier((mine, from_core[1]))
        from_core[s] = over_core(mine)

    def chip_tokens(s, h):
        return jnp.concatenate([own_tokens(s, h, core), from_core[s][h * tokens : (h + 1) * tokens]], axis=0)

    bits = [1 << i for i in range((n_tensor - 1).bit_length())]
    ways = []
    for q in range(2):
        partner = bits[q]
        gather = [bit for bit in bits if bit != partner]
        at = [0]
        for bit in gather:
            at = at + [m ^ bit for m in at]
        ways.append((partner, gather, at))

    def rows_of(array, mine):
        return lax.dynamic_slice(array, (mine * tokens, 0), (tokens, array.shape[1]))

    kv_other = over_core(kv_grad)
    kv_mine, kv_theirs = [], []
    for partner, gather, at in ways:
        kv_mine.append(
            jnp.concatenate(
                [rows_of(array, me ^ m) for m in at for array in (kv_grad, kv_other)], axis=0
            )
        )
        mine = jnp.concatenate([rows_of(kv_grad, me ^ partner ^ m) for m in at], axis=0)
        got = over_tensor(mine, partner)
        other = over_core(got)
        kv_theirs.append(
            jnp.concatenate(
                [array[i * tokens : (i + 1) * tokens] for i in range(len(at)) for array in (got, other)],
                axis=0,
            )
        )

    arrived = {}
    for s in steps:
        for h in range(2):
            partner, gather, at = ways[h]
            piece = chip_tokens(s, h)
            if s > 1:
                before = arrived[(s - 1, h)]
                piece, before[-1] = lax.optimization_barrier((piece, before[-1]))
            pieces = [piece]
            for bit in gather:
                pieces = pieces + [over_tensor(p, bit) for p in pieces]
            arrived[(s, h)] = pieces

    passed = {}
    grads, squares = [], []
    for s in steps:
        for h in range(2):
            partner = ways[h][0]
            pieces = arrived[(s, h)]
            messages = [over_tensor(run_chunk(pieces, kv_theirs[h], [], "send"), partner)]
            if s > 1:
                messages.append(passed[h])
            if s < n_z:
                passed[h] = hand_on(run_chunk(pieces, kv_mine[h], messages, "send"), h)
            else:
                grad, square = run_chunk(pieces, kv_mine[h], messages, "final")
                grads.append(grad)
                squares.append(square)

    square = squares[0] + squares[1]
    square = square + over_core(square)
    square = square + sum(over_tensor(square, m) for m in range(1, n_tensor))
    square = square + sum(over_z(square, k) for k in range(1, n_z))
    square_sum = jnp.sum(square)
    gradient = jnp.concatenate(grads, axis=0)
    return adam_update(gradient, square_sum, master, first, second, clip_limit)


def solution(mesh):
    in_specs = (
        P(("dp", "tensor"), None),
        P("dp", "tensor"),
        P("dp", "tensor"),
        P("dp", "tensor"),
        P("dp", "tensor"),
        P(),
    )
    out_specs = (P("dp", "tensor"), P("dp", "tensor"), P("dp", "tensor"))
    return jax.shard_map(
        functools.partial(on_device, mesh.shape["dp"], mesh.shape["tensor"]),
        mesh=mesh,
        in_specs=in_specs,
        out_specs=out_specs,
        check_vma=False,
    )
```

```python
import functools

import jax
import jax.numpy as jnp
from jax import lax
from jax.experimental import pallas as pl
from jax.experimental.pallas import tpu as pltpu
from jax.sharding import PartitionSpec as P

STEP = 20

beta_first = 0.9
beta_second = 0.95
learn_rate = 0.00015
decay_rate = 0.1

AXES = ("dp", "tensor")
SCALE_ROWS = 16
KNEE = 64.0
POWER = 32
SHIFT = 3.5
VMEM = 40 * 1024 * 1024


def encode(values, scale):
    u = jnp.abs(values) * (KNEE / jnp.maximum(scale, 1e-30))
    w = (u + jnp.sqrt(u * u + 1.0)) * (2.0**-SHIFT)
    power = 1
    while power < POWER:
        w = w * w
        power *= 2
    return jnp.where(values < 0, -w, w).astype(jnp.bfloat16)


def decode(code, scale):
    code = code.astype(jnp.float32)
    log_w = jnp.log(jnp.maximum(jnp.abs(code), 2.0 ** (-SHIFT * POWER))) * (1.0 / POWER) + SHIFT * 0.6931471805599453
    u = jnp.exp(log_w) - jnp.exp(-log_w)
    size = u * (scale * (0.5 / KNEE))
    return jnp.where(code < 0, -size, size)


def tile_rows(rows):
    return 128 if rows % 128 == 0 else rows


def chunk_kernel(parts, n_arrays, n_in, mode, *refs):
    me = refs[0][0]
    array_refs, in_refs, rest = refs[1 : 1 + n_arrays], refs[1 + n_arrays : 1 + n_arrays + n_in], refs[1 + n_arrays + n_in :]
    (first_a, _, first_b, _, depth, _) = parts[0]
    rows, width = array_refs[first_a].shape[1], array_refs[first_b].shape[1]
    tile = tile_rows(rows)

    def values(at):
        total = None
        for a, a_row, b, b_row, depth, distance in parts:
            if distance is not None:
                b_row = pl.multiple_of((me ^ distance) * depth, 16)
            part = lax.dot_general(
                array_refs[a][pl.ds(a_row, depth), pl.ds(at, tile)],
                array_refs[b][pl.ds(b_row, depth), :],
                (((0,), (0,)), ((), ())),
                preferred_element_type=jnp.float32,
            )
            total = part if total is None else total + part
        for ref in in_refs:
            scale = ref[rows : rows + 1, :].astype(jnp.float32)
            total = total + decode(ref[pl.ds(at, tile), :], scale)
        return total

    if mode == "final":
        out_ref, square_ref = rest[-2:]
        square = jnp.zeros((8, width), jnp.float32)
        for at in range(0, rows, tile):
            total = values(at)
            out_ref[pl.ds(at, tile), :] = total
            square = square + jnp.sum((total * total).reshape(tile // 8, 8, width), axis=0)
        square_ref[...] = sum(square[:, s : s + 128] for s in range(0, width, 128))
        return
    out_ref, held = rest[-2:]
    largest = jnp.zeros((8, width), jnp.float32)
    for at in range(0, rows, tile):
        total = values(at)
        held[pl.ds(at, tile), :] = total
        largest = jnp.maximum(largest, jnp.max(jnp.abs(total).reshape(tile // 8, 8, width), axis=0))
    scale = jnp.max(largest, axis=0, keepdims=True).astype(jnp.bfloat16)
    out_ref[pl.ds(rows, SCALE_ROWS), :] = jnp.broadcast_to(scale, (SCALE_ROWS, width))
    scale = scale.astype(jnp.float32)
    for at in range(0, rows, tile):
        out_ref[pl.ds(at, tile), :] = encode(held[pl.ds(at, tile), :], scale)


def run_chunk(me, arrays, parts, messages, after, mode):
    rows, width = arrays[parts[0][0]].shape[1], arrays[parts[0][2]].shape[1]
    if mode == "final":
        out_shape = (
            jax.ShapeDtypeStruct((rows, width), jnp.float32),
            jax.ShapeDtypeStruct((8, 128), jnp.float32),
        )
        scratch = []
    else:
        out_shape = jax.ShapeDtypeStruct((rows + SCALE_ROWS, width), jnp.bfloat16)
        scratch = [pltpu.VMEM((rows, width), jnp.float32)]
    cost = pl.CostEstimate(flops=1024, bytes_accessed=1024, transcendentals=0)
    whole = pl.BlockSpec(memory_space=pltpu.VMEM)
    return pl.pallas_call(
        functools.partial(chunk_kernel, parts, len(arrays), len(messages), mode),
        out_shape=out_shape,
        in_specs=[pl.BlockSpec(memory_space=pltpu.SMEM)]
        + [whole] * (len(arrays) + len(messages))
        + [pl.BlockSpec(memory_space=pl.ANY)] * len(after),
        scratch_shapes=scratch,
        cost_estimate=cost,
        compiler_params=pltpu.CompilerParams(vmem_limit_bytes=VMEM),
    )(me, *arrays, *messages, *after)


def pack_kernel(copies, where, inputs, kv_grad, behind, *outs):
    for source, index, out, row, rows, column, columns in copies:
        to = outs[out].at[pl.ds(row, rows), pl.ds(column, columns)]
        if source == "columns":
            to[...] = inputs[:, pl.ds(pl.multiple_of(where[index], 128), columns)]
        else:
            to[...] = kv_grad[pl.ds(pl.multiple_of(where[index], 16), rows), :]


def pack(where, inputs, kv_grad, copies, shapes, behind):
    whole = pl.BlockSpec(memory_space=pltpu.VMEM)
    return pl.pallas_call(
        functools.partial(pack_kernel, copies),
        out_shape=[jax.ShapeDtypeStruct(shape, jnp.bfloat16) for shape in shapes],
        in_specs=[pl.BlockSpec(memory_space=pltpu.SMEM), whole, whole, pl.BlockSpec(memory_space=pl.ANY)],
        out_specs=[whole] * len(shapes),
        cost_estimate=pl.CostEstimate(flops=1024, bytes_accessed=1024, transcendentals=0),
        compiler_params=pltpu.CompilerParams(vmem_limit_bytes=VMEM),
    )(where, inputs, kv_grad, behind)


def adam_kernel(n_grads, n_squares, *refs):
    clip_limit = refs[0]
    grads = refs[1 : 1 + n_grads]
    squares = refs[1 + n_grads : 1 + n_grads + n_squares]
    state = refs[1 + n_grads + n_squares :][:3]
    outs = refs[4 + n_grads + n_squares :][:3]
    held, sems = refs[-2:]
    square_sum = squares[0][...]
    for square in squares[1:]:
        square_sum = square_sum + square[...]
    grad_norm = jnp.sqrt(jnp.sum(square_sum, keepdims=True))
    clip_factor = jnp.minimum(1.0, clip_limit[0] / (grad_norm + 1e-06))
    start = 0
    copies = []
    for grad in grads:
        tile = tile_rows(grad.shape[0])
        for at in range(0, grad.shape[0], tile):
            here = pl.ds(start, tile)
            master, first, second = [ref[here, :] for ref in state]
            scaled = grad[pl.ds(at, tile), :] * clip_factor
            new_first = beta_first * first + (1.0 - beta_first) * scaled
            new_second = beta_second * second + (1.0 - beta_second) * scaled * scaled
            first_hat = new_first * (1.0 / (1.0 - beta_first**STEP))
            second_hat = new_second * (1.0 / (1.0 - beta_second**STEP))
            new_master = master - learn_rate * (
                first_hat / (jnp.sqrt(second_hat) + 1e-08) + decay_rate * master
            )
            for i, value in enumerate((new_master, new_first, new_second)):
                held[i, here, :] = value
                copy = pltpu.make_async_copy(held.at[i, here, :], outs[i].at[here, :], sems.at[len(copies)])
                copy.start()
                copies.append(copy)
            start += tile
    for copy in copies:
        copy.wait()


def adam_update(grads, squares, master, first, second, clip_limit):
    whole = pl.BlockSpec(memory_space=pltpu.VMEM)
    n_copies = 3 * sum(grad.shape[0] // tile_rows(grad.shape[0]) for grad in grads)
    return pl.pallas_call(
        functools.partial(adam_kernel, len(grads), len(squares)),
        out_shape=[jax.ShapeDtypeStruct(master.shape, jnp.float32)] * 3,
        in_specs=[pl.BlockSpec(memory_space=pltpu.SMEM)] + [whole] * (len(grads) + len(squares) + 3),
        out_specs=[pl.BlockSpec(memory_space=pl.ANY)] * 3,
        scratch_shapes=[
            pltpu.VMEM((3, *master.shape), jnp.float32),
            pltpu.SemaphoreType.DMA((n_copies,)),
        ],
        cost_estimate=pl.CostEstimate(flops=1024, bytes_accessed=1024, transcendentals=0),
        compiler_params=pltpu.CompilerParams(vmem_limit_bytes=VMEM),
    )(clip_limit, *grads, *squares, master, first, second)


def on_device(n_dp, n_tensor, inputs, kv_grad, master, first, second, clip_limit):
    n_z = n_dp // 2
    dp, me = lax.axis_index("dp"), lax.axis_index("tensor")
    z, core = dp // 2, dp % 2
    tokens, block = inputs.shape[0], master.shape[0]
    widths = [block * 3 // 8, block * 5 // 8] if block % 1024 == 7 else [block // 2] * 2
    offsets = [0, widths[0]]

    def send(x, move):
        pairs = []
        for g in range(n_dp):
            for t in range(n_tensor):
                to = move(g // 2, g % 2, t)
                if to is not None:
                    pairs.append((g * n_tensor + t, (to[0] * 2 + to[1]) * n_tensor + to[2]))
        return lax.ppermute(x, AXES, pairs)

    def over_core(x):
        return send(x, lambda z, c, t: (z, 1 - c, t))

    def over_tensor(x, bit):
        return send(x, lambda z, c, t: (z, c, t ^ bit))

    def over_z(x, bits):
        return send(x, lambda z, c, t: (z ^ bits, c, t))

    def place_of(z):
        return jnp.where(z % 2 == 0, z // 2, n_z - (z + 1) // 2)

    def at_place(place):
        place = place % n_z
        return jnp.where(place < (n_z + 1) // 2, 2 * place, 2 * (n_z - place) - 1)

    ring = list(range(0, n_z, 2)) + list(range(n_z - 1 - n_z % 2, 0, -2))
    ways_round = (1, -1)

    def hand_on(x, h):
        return send(x, lambda z, c, t: (ring[(ring.index(z) + ways_round[h]) % n_z], c, t))

    def columns(s, owner_core, h):
        owner = at_place(place_of(z) - ways_round[h] * s)
        return (owner * 2 + owner_core) * block + offsets[h]

    steps = list(range(1, n_z + 1))

    def after(x, *others):
        return lax.optimization_barrier((x, *others))[0]

    bits = [1 << i for i in range((n_tensor - 1).bit_length())]
    ways = []
    for q in range(2):
        partner = bits[q]
        gather = [bit for bit in bits if bit != partner]
        at = [0]
        for bit in gather:
            at = at + [m ^ bit for m in at]
        ways.append((partner, gather, at))

    pieces = [(s, h) for s in steps for h in range(2)]
    where = [columns(s, core, h) for s, h in pieces] + [columns(s, 1 - core, h) for s, h in pieces]
    where += [(me ^ partner ^ m) * tokens for partner, _, at in ways for m in at]
    where = jnp.stack(where).astype(jnp.int32)
    n, n_at = len(pieces), len(ways[0][2])
    shapes = [(tokens, block)] + [(n_at * tokens, kv_grad.shape[1])] * 2 + [(tokens, width) for width in widths]
    copies = [("columns", n + h, 0, 0, tokens, offsets[h], widths[h]) for h in range(2)]
    copies += [
        ("rows", 2 * n + q * n_at + i, 1 + q, i * tokens, tokens, 0, kv_grad.shape[1])
        for q in range(2)
        for i in range(n_at)
    ]
    copies += [("columns", h, 3 + h, 0, tokens, 0, widths[h]) for h in range(2)]
    soon_out, kv_out0, kv_out1, *own = pack(where, inputs, kv_grad, copies, shapes, where)
    shapes = [((n_z - 1) * tokens, block)] + [(tokens, widths[h]) for _, h in pieces[2:]]
    copies = [
        ("columns", n + i, 0, (s - 2) * tokens, tokens, offsets[h], widths[h])
        for i, (s, h) in enumerate(pieces)
        if s > 1
    ]
    copies += [("columns", i, i - 1, 0, tokens, 0, widths[h]) for i, (s, h) in enumerate(pieces) if s > 1]
    later_out, *own_then = pack(where, inputs, kv_grad, copies, shapes, soon_out)
    own = dict(zip(pieces, own + own_then))

    soon = over_core(soon_out)
    kv_partner = [over_tensor(kv_out0, ways[0][0]), over_tensor(kv_out1, ways[1][0])]

    def chip_tokens(s, h):
        other = soon if s == 1 else later[(s - 2) * tokens : (s - 1) * tokens]
        return jnp.concatenate([own[(s, h)], other[:, offsets[h] : offsets[h] + widths[h]]], axis=0)

    def gather(piece, h):
        pieces = [piece]
        for bit in ways[h][1]:
            pieces = pieces + [over_tensor(p, bit) for p in pieces]
        return pieces

    arrived = {(1, 0): gather(chip_tokens(1, 0), 0)}
    arrived[(1, 1)] = gather(chip_tokens(1, 1), 1)
    kv_partner_other = [over_core(after(kv_partner[h], *arrived[(1, h)][1:])) for h in range(2)]

    my_index = jnp.reshape(me, (1,)).astype(jnp.int32)

    def partner_part(s, h, behind):
        pieces = arrived[(s, h)]
        n = len(pieces)
        parts = [
            (i, c * tokens, n + c, i * tokens, tokens, None) for i in range(n) for c in range(2)
        ]
        return run_chunk(
            my_index, [*pieces, kv_partner[h], kv_partner_other[h]], parts, [], behind, "send"
        )

    def own_part(s, h, messages, behind, mode):
        pieces = arrived[(s, h)]
        n = len(pieces)
        parts = [
            (i, c * tokens, n + c, 0, tokens, ways[h][2][i]) for i in range(n) for c in range(2)
        ]
        return run_chunk(my_index, [*pieces, kv_grad, kv_other], parts, messages, behind, mode)

    order = [("partner", 1, 0), ("partner", 1, 1)]
    for s in steps:
        for h in range(2):
            order.append(("own", s, h))
            if s < n_z:
                order.append(("partner", s + 1, h))
    starts_gather = {("partner", 1, 0): (2, 0), ("partner", 1, 1): (2, 1)}
    for s in steps:
        starts_gather[("own", s, 1)] = (s + 2, 0)
        if s > 1:
            starts_gather[("own", s, 0)] = (s + 1, 1)
    behind = arrived[(1, 1)][1:] + kv_partner_other[1:]
    from_partner, passed, grads, squares = {}, {}, [], []
    later = None
    for kind, s, h in order:
        if kind == "partner":
            out = partner_part(s, h, behind)
            from_partner[(s, h)] = over_tensor(out, ways[h][0])
        else:
            messages = [from_partner[(s, h)]] + ([passed[h]] if s > 1 else [])
            if s < n_z:
                out = own_part(s, h, messages, behind, "send")
                passed[h] = hand_on(out, h)
            else:
                grad, out = own_part(s, h, messages, behind, "final")
                grads.append(grad)
                squares.append(out)
        behind = [out]
        if later is None:
            later = over_core(after(later_out, out))
            kv_other = over_core(after(kv_grad, later))
        if (kind, s, h) in starts_gather and starts_gather[(kind, s, h)][0] <= n_z:
            then, half_then = starts_gather[(kind, s, h)]
            arrived[(then, half_then)] = gather(after(chip_tokens(then, half_then), out), half_then)

    square = squares[0] + squares[1]
    square = square + over_core(square)
    square = square + sum(over_tensor(square, m) for m in range(1, n_tensor))
    squares = [square] + [over_z(square, k) for k in range(1, n_z)]
    return tuple(adam_update(grads, squares, master, first, second, clip_limit))


def solution(mesh):
    in_specs = (
        P(("dp", "tensor"), None),
        P("dp", "tensor"),
        P("dp", "tensor"),
        P("dp", "tensor"),
        P("dp", "tensor"),
        P(),
    )
    out_specs = (P("dp", "tensor"), P("dp", "tensor"), P("dp", "tensor"))
    return jax.shard_map(
        functools.partial(on_device, mesh.shape["dp"], mesh.shape["tensor"]),
        mesh=mesh,
        in_specs=in_specs,
        out_specs=out_specs,
        check_vma=False,
    )
```

```python
import functools

import jax
import jax.numpy as jnp
from jax import lax
from jax.experimental import pallas as pl
from jax.experimental.pallas import tpu as pltpu
from jax.sharding import PartitionSpec as P

STEP = 20

beta_first = 0.9
beta_second = 0.95
learn_rate = 0.00015
decay_rate = 0.1

AXES = ("dp", "tensor")
SCALE_ROWS = 16
KNEE = 64.0
POWER = 32
SHIFT = 3.5
VMEM = 40 * 1024 * 1024

CONFIG = dict(e=(1, -1) * 3, g=(3, 3) * 3, z=(0,) * 6, a=(0,) * 6, split=4, start=0, bgate=0, later=0)


def encode(values, scale):
    u = jnp.abs(values) * (KNEE / jnp.maximum(scale, 1e-30))
    w = (u + jnp.sqrt(u * u + 1.0)) * (2.0**-SHIFT)
    power = 1
    while power < POWER:
        w = w * w
        power *= 2
    return jnp.where(values < 0, -w, w).astype(jnp.bfloat16)


def decode(code, scale):
    code = code.astype(jnp.float32)
    log_w = jnp.log(jnp.maximum(jnp.abs(code), 2.0 ** (-SHIFT * POWER))) * (1.0 / POWER) + SHIFT * 0.6931471805599453
    u = jnp.exp(log_w) - jnp.exp(-log_w)
    size = u * (scale * (0.5 / KNEE))
    return jnp.where(code < 0, -size, size)


def tile_rows(rows):
    return 128 if rows % 128 == 0 else rows


def chunk_kernel(parts, n_arrays, n_in, mode, *refs):
    me = refs[0][0]
    array_refs, in_refs, rest = refs[1 : 1 + n_arrays], refs[1 + n_arrays : 1 + n_arrays + n_in], refs[1 + n_arrays + n_in :]
    (first_a, _, first_b, _, depth, _) = parts[0]
    rows, width = array_refs[first_a].shape[1], array_refs[first_b].shape[1]
    tile = tile_rows(rows)

    def values(at):
        total = None
        for a, a_row, b, b_row, depth, distance in parts:
            if distance is not None:
                b_row = pl.multiple_of((me ^ distance) * depth, 16)
            part = lax.dot_general(
                array_refs[a][pl.ds(a_row, depth), pl.ds(at, tile)],
                array_refs[b][pl.ds(b_row, depth), :],
                (((0,), (0,)), ((), ())),
                preferred_element_type=jnp.float32,
            )
            total = part if total is None else total + part
        for ref in in_refs:
            scale = ref[rows : rows + 1, :].astype(jnp.float32)
            total = total + decode(ref[pl.ds(at, tile), :], scale)
        return total

    if mode == "final":
        out_ref, square_ref = rest[-2:]
        square = jnp.zeros((8, width), jnp.float32)
        for at in range(0, rows, tile):
            total = values(at)
            out_ref[pl.ds(at, tile), :] = total
            square = square + jnp.sum((total * total).reshape(tile // 8, 8, width), axis=0)
        square_ref[...] = sum(square[:, s : s + 128] for s in range(0, width, 128))
        return
    out_ref, held = rest[-2:]
    largest = jnp.zeros((8, width), jnp.float32)
    for at in range(0, rows, tile):
        total = values(at)
        held[pl.ds(at, tile), :] = total
        largest = jnp.maximum(largest, jnp.max(jnp.abs(total).reshape(tile // 8, 8, width), axis=0))
    scale = jnp.max(largest, axis=0, keepdims=True).astype(jnp.bfloat16)
    out_ref[pl.ds(rows, SCALE_ROWS), :] = jnp.broadcast_to(scale, (SCALE_ROWS, width))
    scale = scale.astype(jnp.float32)
    for at in range(0, rows, tile):
        out_ref[pl.ds(at, tile), :] = encode(held[pl.ds(at, tile), :], scale)


def run_chunk(me, arrays, parts, messages, after, mode):
    rows, width = arrays[parts[0][0]].shape[1], arrays[parts[0][2]].shape[1]
    if mode == "final":
        out_shape = (
            jax.ShapeDtypeStruct((rows, width), jnp.float32),
            jax.ShapeDtypeStruct((8, 128), jnp.float32),
        )
        scratch = []
    else:
        out_shape = jax.ShapeDtypeStruct((rows + SCALE_ROWS, width), jnp.bfloat16)
        scratch = [pltpu.VMEM((rows, width), jnp.float32)]
    cost = pl.CostEstimate(flops=1024, bytes_accessed=1024, transcendentals=0)
    whole = pl.BlockSpec(memory_space=pltpu.VMEM)
    return pl.pallas_call(
        functools.partial(chunk_kernel, parts, len(arrays), len(messages), mode),
        out_shape=out_shape,
        in_specs=[pl.BlockSpec(memory_space=pltpu.SMEM)]
        + [whole] * (len(arrays) + len(messages))
        + [pl.BlockSpec(memory_space=pl.ANY)] * len(after),
        scratch_shapes=scratch,
        cost_estimate=cost,
        compiler_params=pltpu.CompilerParams(vmem_limit_bytes=VMEM),
    )(me, *arrays, *messages, *after)


def pack_kernel(copies, where, inputs, kv_grad, behind, *outs):
    for source, index, out, row, rows, column, columns in copies:
        to = outs[out].at[pl.ds(row, rows), pl.ds(column, columns)]
        if source == "columns":
            to[...] = inputs[:, pl.ds(pl.multiple_of(where[index], 128), columns)]
        else:
            to[...] = kv_grad[pl.ds(pl.multiple_of(where[index], 16), rows), :]


def pack(where, inputs, kv_grad, copies, shapes, behind):
    whole = pl.BlockSpec(memory_space=pltpu.VMEM)
    return pl.pallas_call(
        functools.partial(pack_kernel, copies),
        out_shape=[jax.ShapeDtypeStruct(shape, jnp.bfloat16) for shape in shapes],
        in_specs=[pl.BlockSpec(memory_space=pltpu.SMEM), whole, whole, pl.BlockSpec(memory_space=pl.ANY)],
        out_specs=[whole] * len(shapes),
        cost_estimate=pl.CostEstimate(flops=1024, bytes_accessed=1024, transcendentals=0),
        compiler_params=pltpu.CompilerParams(vmem_limit_bytes=VMEM),
    )(where, inputs, kv_grad, behind)


def adam_kernel(n_grads, n_squares, *refs):
    clip_limit = refs[0]
    grads = refs[1 : 1 + n_grads]
    squares = refs[1 + n_grads : 1 + n_grads + n_squares]
    state = refs[1 + n_grads + n_squares :][:3]
    outs = refs[4 + n_grads + n_squares :][:3]
    held, sems = refs[-2:]
    square_sum = squares[0][...]
    for square in squares[1:]:
        square_sum = square_sum + square[...]
    grad_norm = jnp.sqrt(jnp.sum(square_sum, keepdims=True))
    clip_factor = jnp.minimum(1.0, clip_limit[0] / (grad_norm + 1e-06))
    start = 0
    copies = []
    for grad in grads:
        tile = tile_rows(grad.shape[0])
        for at in range(0, grad.shape[0], tile):
            here = pl.ds(start, tile)
            master, first, second = [ref[here, :] for ref in state]
            scaled = grad[pl.ds(at, tile), :] * clip_factor
            new_first = beta_first * first + (1.0 - beta_first) * scaled
            new_second = beta_second * second + (1.0 - beta_second) * scaled * scaled
            first_hat = new_first * (1.0 / (1.0 - beta_first**STEP))
            second_hat = new_second * (1.0 / (1.0 - beta_second**STEP))
            new_master = master - learn_rate * (
                first_hat / (jnp.sqrt(second_hat) + 1e-08) + decay_rate * master
            )
            for i, value in enumerate((new_master, new_first, new_second)):
                held[i, here, :] = value
                copy = pltpu.make_async_copy(held.at[i, here, :], outs[i].at[here, :], sems.at[len(copies)])
                copy.start()
                copies.append(copy)
            start += tile
    for copy in copies:
        copy.wait()


def adam_update(grads, squares, master, first, second, clip_limit):
    whole = pl.BlockSpec(memory_space=pltpu.VMEM)
    n_copies = 3 * sum(grad.shape[0] // tile_rows(grad.shape[0]) for grad in grads)
    return pl.pallas_call(
        functools.partial(adam_kernel, len(grads), len(squares)),
        out_shape=[jax.ShapeDtypeStruct(master.shape, jnp.float32)] * 3,
        in_specs=[pl.BlockSpec(memory_space=pltpu.SMEM)] + [whole] * (len(grads) + len(squares) + 3),
        out_specs=[pl.BlockSpec(memory_space=pl.ANY)] * 3,
        scratch_shapes=[
            pltpu.VMEM((3, *master.shape), jnp.float32),
            pltpu.SemaphoreType.DMA((n_copies,)),
        ],
        cost_estimate=pl.CostEstimate(flops=1024, bytes_accessed=1024, transcendentals=0),
        compiler_params=pltpu.CompilerParams(vmem_limit_bytes=VMEM),
    )(clip_limit, *grads, *squares, master, first, second)


def on_device(n_dp, n_tensor, inputs, kv_grad, master, first, second, clip_limit):
    n_z = n_dp // 2
    dp, me = lax.axis_index("dp"), lax.axis_index("tensor")
    z, core = dp // 2, dp % 2
    tokens, block = inputs.shape[0], master.shape[0]
    widths = [block * CONFIG['split'] // 8, block - block * CONFIG['split'] // 8] if block % 1024 == 0 else [block // 2] * 2
    offsets = [0, widths[0]]

    def send(x, move):
        pairs = []
        for g in range(n_dp):
            for t in range(n_tensor):
                to = move(g // 2, g % 2, t)
                if to is not None:
                    pairs.append((g * n_tensor + t, (to[0] * 2 + to[1]) * n_tensor + to[2]))
        return lax.ppermute(x, AXES, pairs)

    def over_core(x):
        return send(x, lambda z, c, t: (z, 1 - c, t))

    def over_tensor(x, bit):
        return send(x, lambda z, c, t: (z, c, t ^ bit))

    def over_z(x, bits):
        return send(x, lambda z, c, t: (z ^ bits, c, t))

    def place_of(z):
        return jnp.where(z % 2 == 0, z // 2, n_z - (z + 1) // 2)

    def at_place(place):
        place = place % n_z
        return jnp.where(place < (n_z + 1) // 2, 2 * place, 2 * (n_z - place) - 1)

    ring = list(range(0, n_z, 2)) + list(range(n_z - 1 - n_z % 2, 0, -2))
    ways_round = (1, -1)

    def hand_on(x, h):
        return send(x, lambda z, c, t: (ring[(ring.index(z) + ways_round[h]) % n_z], c, t))

    def columns(s, owner_core, h):
        owner = at_place(place_of(z) - ways_round[h] * s)
        return (owner * 2 + owner_core) * block + offsets[h]

    steps = list(range(1, n_z + 1))

    def after(x, *others):
        return lax.optimization_barrier((x, *others))[0]

    bits = [1 << i for i in range((n_tensor - 1).bit_length())]
    ways = []
    for q in range(2):
        partner = bits[q]
        gather = [bit for bit in bits if bit != partner]
        at = [0]
        for bit in gather:
            at = at + [m ^ bit for m in at]
        ways.append((partner, gather, at))

    pieces = [(s, h) for s in steps for h in range(2)]
    where = [columns(s, core, h) for s, h in pieces] + [columns(s, 1 - core, h) for s, h in pieces]
    where += [(me ^ partner ^ m) * tokens for partner, _, at in ways for m in at]
    where = jnp.stack(where).astype(jnp.int32)
    n, n_at = len(pieces), len(ways[0][2])
    shapes = [(tokens, block)] + [(n_at * tokens, kv_grad.shape[1])] * 2 + [(tokens, width) for width in widths]
    copies = [("columns", n + h, 0, 0, tokens, offsets[h], widths[h]) for h in range(2)]
    copies += [
        ("rows", 2 * n + q * n_at + i, 1 + q, i * tokens, tokens, 0, kv_grad.shape[1])
        for q in range(2)
        for i in range(n_at)
    ]
    copies += [("columns", h, 3 + h, 0, tokens, 0, widths[h]) for h in range(2)]
    soon_out, kv_out0, kv_out1, *own = pack(where, inputs, kv_grad, copies, shapes, where)
    shapes = [((n_z - 1) * tokens, block)] + [(tokens, widths[h]) for _, h in pieces[2:]]
    copies = [
        ("columns", n + i, 0, (s - 2) * tokens, tokens, offsets[h], widths[h])
        for i, (s, h) in enumerate(pieces)
        if s > 1
    ]
    copies += [("columns", i, i - 1, 0, tokens, 0, widths[h]) for i, (s, h) in enumerate(pieces) if s > 1]
    later_out, *own_then = pack(where, inputs, kv_grad, copies, shapes, soon_out)
    own = dict(zip(pieces, own + own_then))

    soon = over_core(soon_out)
    if CONFIG['bgate']:
        kv_out0, kv_out1 = after(kv_out0, soon), after(kv_out1, soon)
    kv_partner = [over_tensor(kv_out0, ways[0][0]), over_tensor(kv_out1, ways[1][0])]

    def chip_tokens(s, h):
        other = soon if s == 1 else later[(s - 2) * tokens : (s - 1) * tokens]
        return jnp.concatenate([own[(s, h)], other[:, offsets[h] : offsets[h] + widths[h]]], axis=0)

    def gather(piece, h):
        pieces = [piece]
        for bit in ways[h][1]:
            pieces = pieces + [over_tensor(p, bit) for p in pieces]
        return pieces

    arrived = {(1, 0): gather(chip_tokens(1, 0), 0)}
    arrived[(1, 1)] = gather(chip_tokens(1, 1), 1)
    waits = [[], [soon], None][CONFIG['start']]
    kv_partner_other = [
        over_core(after(kv_partner[h], *(arrived[(1, h)][1:] if waits is None else waits)))
        for h in range(2)
    ]

    my_index = jnp.reshape(me, (1,)).astype(jnp.int32)

    def partner_part(s, h, behind):
        pieces = arrived[(s, h)]
        n = len(pieces)
        parts = [
            (i, c * tokens, n + c, i * tokens, tokens, None) for i in range(n) for c in range(2)
        ]
        return run_chunk(
            my_index, [*pieces, kv_partner[h], kv_partner_other[h]], parts, [], behind, "send"
        )

    def own_part(s, h, messages, behind, mode):
        pieces = arrived[(s, h)]
        n = len(pieces)
        parts = [
            (i, c * tokens, n + c, 0, tokens, ways[h][2][i]) for i in range(n) for c in range(2)
        ]
        return run_chunk(my_index, [*pieces, kv_grad, kv_other], parts, messages, behind, mode)

    def chosen(name, s, h):
        return CONFIG[name][2 * (min(s, 4) - 2) + h]

    keyed = [(4 * s + 2 * h, ("own", s, h)) for s in steps for h in range(2)]
    keyed += [(4 * (s - 1) + 2 * h + (chosen("e", s, h) if s > 1 else -3) + 0.1 * h, ("partner", s, h)) for s in steps for h in range(2)]
    order = [kernel for _, kernel in sorted(keyed)]
    place = {kernel: i for i, kernel in enumerate(order)}
    released = {i: [] for i in range(len(order))}
    for s in steps[1:]:
        for h in range(2):
            released[max(place[("partner", s, h)] - chosen("g", s, h), CONFIG['later'])].append((s, h))
    behind = arrived[(1, 1)][1:] + kv_partner_other[1:]
    from_partner, passed, grads, squares = {}, {}, [], []
    for i, (kind, s, h) in enumerate(order):
        if kind == "partner" and s > 1 and chosen("z", s, h):
            ready = [passed[key] for key in [(1 - h, s - 1), (1 - h, s - 2)] if key in passed]
            behind = behind + ready[:1]
        if kind == "own" and 1 < s and chosen("a", s, h) and (s + 1, h) in arrived:
            behind = behind + arrived[(s + 1, h)][1:]
        if kind == "partner":
            out = partner_part(s, h, behind)
            from_partner[(s, h)] = over_tensor(out, ways[h][0])
        else:
            messages = [from_partner[(s, h)]] + ([passed[(h, s - 1)]] if s > 1 else [])
            if s < n_z:
                out = own_part(s, h, messages, behind, "send")
                passed[(h, s)] = hand_on(out, h)
            else:
                grad, out = own_part(s, h, messages, behind, "final")
                grads.append(grad)
                squares.append(out)
        behind = [out]
        if i == CONFIG['later']:
            later = over_core(after(later_out, out))
            kv_other = over_core(after(kv_grad, later))
        for then, half_then in released[i]:
            arrived[(then, half_then)] = gather(after(chip_tokens(then, half_then), out), half_then)

    square = squares[0] + squares[1]
    square = square + over_core(square)
    square = square + sum(over_tensor(square, m) for m in range(1, n_tensor))
    squares = [square] + [over_z(square, k) for k in range(1, n_z)]
    return tuple(adam_update(grads, squares, master, first, second, clip_limit))


def solution(mesh):
    in_specs = (
        P(("dp", "tensor"), None),
        P("dp", "tensor"),
        P("dp", "tensor"),
        P("dp", "tensor"),
        P("dp", "tensor"),
        P(),
    )
    out_specs = (P("dp", "tensor"), P("dp", "tensor"), P("dp", "tensor"))
    return jax.shard_map(
        functools.partial(on_device, mesh.shape["dp"], mesh.shape["tensor"]),
        mesh=mesh,
        in_specs=in_specs,
        out_specs=out_specs,
        check_vma=False,
    )
```

```python
import functools

import jax
import jax.numpy as jnp
from jax import lax
from jax.experimental import pallas as pl
from jax.experimental.pallas import tpu as pltpu
from jax.sharding import PartitionSpec as P

STEP = 20

beta_first = 0.9
beta_second = 0.95
learn_rate = 0.00015
decay_rate = 0.1

AXES = ("dp", "tensor")
SCALE_ROWS = 16
KNEE = 64.0
POWER = 32
SHIFT = 3.5
VMEM = 40 * 1024 * 1024

PARTNER_PLACE = (1, -1)
GATHER_AHEAD = {2: (2, 3), 3: (3, 3)}


def encode(values, scale):
    u = jnp.abs(values) * (KNEE / jnp.maximum(scale, 1e-30))
    w = (u + jnp.sqrt(u * u + 1.0)) * (2.0**-SHIFT)
    power = 1
    while power < POWER:
        w = w * w
        power *= 2
    return jnp.where(values < 0, -w, w).astype(jnp.bfloat16)


def decode(code, scale):
    code = code.astype(jnp.float32)
    log_w = jnp.log(jnp.maximum(jnp.abs(code), 2.0 ** (-SHIFT * POWER))) * (1.0 / POWER) + SHIFT * 0.6931471805599453
    u = jnp.exp(log_w) - jnp.exp(-log_w)
    size = u * (scale * (0.5 / KNEE))
    return jnp.where(code < 0, -size, size)


def tile_rows(rows):
    return 128 if rows % 128 == 0 else rows


def chunk_kernel(parts, n_arrays, n_in, mode, *refs):
    me = refs[0][0]
    array_refs, in_refs, rest = refs[1 : 1 + n_arrays], refs[1 + n_arrays : 1 + n_arrays + n_in], refs[1 + n_arrays + n_in :]
    (first_a, _, first_b, _, depth, _) = parts[0]
    rows, width = array_refs[first_a].shape[1], array_refs[first_b].shape[1]
    tile = tile_rows(rows)

    def values(at):
        total = None
        for a, a_row, b, b_row, depth, distance in parts:
            if distance is not None:
                b_row = pl.multiple_of((me ^ distance) * depth, 16)
            part = lax.dot_general(
                array_refs[a][pl.ds(a_row, depth), pl.ds(at, tile)],
                array_refs[b][pl.ds(b_row, depth), :],
                (((0,), (0,)), ((), ())),
                preferred_element_type=jnp.float32,
            )
            total = part if total is None else total + part
        for ref in in_refs:
            scale = ref[rows : rows + 1, :].astype(jnp.float32)
            total = total + decode(ref[pl.ds(at, tile), :], scale)
        return total

    if mode == "final":
        out_ref, square_ref = rest[-2:]
        square = jnp.zeros((8, width), jnp.float32)
        for at in range(0, rows, tile):
            total = values(at)
            out_ref[pl.ds(at, tile), :] = total
            square = square + jnp.sum((total * total).reshape(tile // 8, 8, width), axis=0)
        square_ref[...] = sum(square[:, s : s + 128] for s in range(0, width, 128))
        return
    out_ref, held = rest[-2:]
    largest = jnp.zeros((8, width), jnp.float32)
    for at in range(0, rows, tile):
        total = values(at)
        held[pl.ds(at, tile), :] = total
        largest = jnp.maximum(largest, jnp.max(jnp.abs(total).reshape(tile // 8, 8, width), axis=0))
    scale = jnp.max(largest, axis=0, keepdims=True).astype(jnp.bfloat16)
    out_ref[pl.ds(rows, SCALE_ROWS), :] = jnp.broadcast_to(scale, (SCALE_ROWS, width))
    scale = scale.astype(jnp.float32)
    for at in range(0, rows, tile):
        out_ref[pl.ds(at, tile), :] = encode(held[pl.ds(at, tile), :], scale)


def run_chunk(me, arrays, parts, messages, after, mode):
    rows, width = arrays[parts[0][0]].shape[1], arrays[parts[0][2]].shape[1]
    if mode == "final":
        out_shape = (
            jax.ShapeDtypeStruct((rows, width), jnp.float32),
            jax.ShapeDtypeStruct((8, 128), jnp.float32),
        )
        scratch = []
    else:
        out_shape = jax.ShapeDtypeStruct((rows + SCALE_ROWS, width), jnp.bfloat16)
        scratch = [pltpu.VMEM((rows, width), jnp.float32)]
    cost = pl.CostEstimate(flops=1024, bytes_accessed=1024, transcendentals=0)
    whole = pl.BlockSpec(memory_space=pltpu.VMEM)
    return pl.pallas_call(
        functools.partial(chunk_kernel, parts, len(arrays), len(messages), mode),
        out_shape=out_shape,
        in_specs=[pl.BlockSpec(memory_space=pltpu.SMEM)]
        + [whole] * (len(arrays) + len(messages))
        + [pl.BlockSpec(memory_space=pl.ANY)] * len(after),
        scratch_shapes=scratch,
        cost_estimate=cost,
        compiler_params=pltpu.CompilerParams(vmem_limit_bytes=VMEM),
    )(me, *arrays, *messages, *after)


def pack_kernel(copies, where, inputs, kv_grad, behind, *outs):
    for source, index, out, row, rows, column, columns in copies:
        to = outs[out].at[pl.ds(row, rows), pl.ds(column, columns)]
        if source == "columns":
            to[...] = inputs[:, pl.ds(pl.multiple_of(where[index], 128), columns)]
        else:
            to[...] = kv_grad[pl.ds(pl.multiple_of(where[index], 16), rows), :]


def pack(where, inputs, kv_grad, copies, shapes, behind):
    whole = pl.BlockSpec(memory_space=pltpu.VMEM)
    return pl.pallas_call(
        functools.partial(pack_kernel, copies),
        out_shape=[jax.ShapeDtypeStruct(shape, jnp.bfloat16) for shape in shapes],
        in_specs=[pl.BlockSpec(memory_space=pltpu.SMEM), whole, whole, pl.BlockSpec(memory_space=pl.ANY)],
        out_specs=[whole] * len(shapes),
        cost_estimate=pl.CostEstimate(flops=1024, bytes_accessed=1024, transcendentals=0),
        compiler_params=pltpu.CompilerParams(vmem_limit_bytes=VMEM),
    )(where, inputs, kv_grad, behind)


def adam_kernel(n_grads, n_squares, *refs):
    clip_limit = refs[0]
    grads = refs[1 : 1 + n_grads]
    squares = refs[1 + n_grads : 1 + n_grads + n_squares]
    state = refs[1 + n_grads + n_squares :][:3]
    outs = refs[4 + n_grads + n_squares :][:3]
    held, sems = refs[-2:]
    square_sum = squares[0][...]
    for square in squares[1:]:
        square_sum = square_sum + square[...]
    grad_norm = jnp.sqrt(jnp.sum(square_sum, keepdims=True))
    clip_factor = jnp.minimum(1.0, clip_limit[0] / (grad_norm + 1e-06))
    start = 0
    copies = []
    for grad in grads:
        tile = tile_rows(grad.shape[0])
        for at in range(0, grad.shape[0], tile):
            here = pl.ds(start, tile)
            master, first, second = [ref[here, :] for ref in state]
            scaled = grad[pl.ds(at, tile), :] * clip_factor
            new_first = beta_first * first + (1.0 - beta_first) * scaled
            new_second = beta_second * second + (1.0 - beta_second) * scaled * scaled
            first_hat = new_first * (1.0 / (1.0 - beta_first**STEP))
            second_hat = new_second * (1.0 / (1.0 - beta_second**STEP))
            new_master = master - learn_rate * (
                first_hat / (jnp.sqrt(second_hat) + 1e-08) + decay_rate * master
            )
            for i, value in enumerate((new_master, new_first, new_second)):
                held[i, here, :] = value
                copy = pltpu.make_async_copy(held.at[i, here, :], outs[i].at[here, :], sems.at[len(copies)])
                copy.start()
                copies.append(copy)
            start += tile
    for copy in copies:
        copy.wait()


def adam_update(grads, squares, master, first, second, clip_limit):
    whole = pl.BlockSpec(memory_space=pltpu.VMEM)
    n_copies = 3 * sum(grad.shape[0] // tile_rows(grad.shape[0]) for grad in grads)
    return pl.pallas_call(
        functools.partial(adam_kernel, len(grads), len(squares)),
        out_shape=[jax.ShapeDtypeStruct(master.shape, jnp.float32)] * 3,
        in_specs=[pl.BlockSpec(memory_space=pltpu.SMEM)] + [whole] * (len(grads) + len(squares) + 3),
        out_specs=[pl.BlockSpec(memory_space=pl.ANY)] * 3,
        scratch_shapes=[
            pltpu.VMEM((3, *master.shape), jnp.float32),
            pltpu.SemaphoreType.DMA((n_copies,)),
        ],
        cost_estimate=pl.CostEstimate(flops=1024, bytes_accessed=1024, transcendentals=0),
        compiler_params=pltpu.CompilerParams(vmem_limit_bytes=VMEM),
    )(clip_limit, *grads, *squares, master, first, second)


def on_device(n_dp, n_tensor, inputs, kv_grad, master, first, second, clip_limit):
    n_z = n_dp // 2
    dp, me = lax.axis_index("dp"), lax.axis_index("tensor")
    z, core = dp // 2, dp % 2
    tokens, block = inputs.shape[0], master.shape[0]
    widths = [block // 2] * 2
    offsets = [0, block // 2]

    def send(x, move):
        pairs = []
        for g in range(n_dp):
            for t in range(n_tensor):
                to = move(g // 2, g % 2, t)
                if to is not None:
                    pairs.append((g * n_tensor + t, (to[0] * 2 + to[1]) * n_tensor + to[2]))
        return lax.ppermute(x, AXES, pairs)

    def over_core(x):
        return send(x, lambda z, c, t: (z, 1 - c, t))

    def over_tensor(x, bit):
        return send(x, lambda z, c, t: (z, c, t ^ bit))

    def over_z(x, bits):
        return send(x, lambda z, c, t: (z ^ bits, c, t))

    def place_of(z):
        return jnp.where(z % 2 == 0, z // 2, n_z - (z + 1) // 2)

    def at_place(place):
        place = place % n_z
        return jnp.where(place < (n_z + 1) // 2, 2 * place, 2 * (n_z - place) - 1)

    ring = list(range(0, n_z, 2)) + list(range(n_z - 1 - n_z % 2, 0, -2))
    ways_round = (1, -1)

    def hand_on(x, h):
        return send(x, lambda z, c, t: (ring[(ring.index(z) + ways_round[h]) % n_z], c, t))

    def columns(s, owner_core, h):
        owner = at_place(place_of(z) - ways_round[h] * s)
        return (owner * 2 + owner_core) * block + offsets[h]

    steps = list(range(1, n_z + 1))

    def after(x, *others):
        return lax.optimization_barrier((x, *others))[0]

    bits = [1 << i for i in range((n_tensor - 1).bit_length())]
    ways = []
    for q in range(2):
        partner = bits[q]
        gather = [bit for bit in bits if bit != partner]
        at = [0]
        for bit in gather:
            at = at + [m ^ bit for m in at]
        ways.append((partner, gather, at))

    pieces = [(s, h) for s in steps for h in range(2)]
    where = [columns(s, core, h) for s, h in pieces] + [columns(s, 1 - core, h) for s, h in pieces]
    where += [(me ^ partner ^ m) * tokens for partner, _, at in ways for m in at]
    where = jnp.stack(where).astype(jnp.int32)
    n, n_at = len(pieces), len(ways[0][2])
    copies = [
        ("rows", 2 * n + q * n_at + i, q, i * tokens, tokens, 0, kv_grad.shape[1])
        for q in range(2)
        for i in range(n_at)
    ]
    kv_out0, kv_out1 = pack(where, kv_grad, kv_grad, copies, [(n_at * tokens, kv_grad.shape[1])] * 2, where)
    shapes = [(tokens, block)] + [(tokens, width) for width in widths]
    copies = [("columns", n + h, 0, 0, tokens, offsets[h], widths[h]) for h in range(2)]
    copies += [("columns", h, 1 + h, 0, tokens, 0, widths[h]) for h in range(2)]
    soon_out, *own = pack(where, inputs, kv_grad, copies, shapes, kv_out0)
    shapes = [((n_z - 1) * tokens, block)] + [(tokens, widths[h]) for _, h in pieces[2:]]
    copies = [
        ("columns", n + i, 0, (s - 2) * tokens, tokens, offsets[h], widths[h])
        for i, (s, h) in enumerate(pieces)
        if s > 1
    ]
    copies += [("columns", i, i - 1, 0, tokens, 0, widths[h]) for i, (s, h) in enumerate(pieces) if s > 1]
    later_out, *own_then = pack(where, inputs, kv_grad, copies, shapes, soon_out)
    own = dict(zip(pieces, own + own_then))

    soon = over_core(soon_out)
    def chip_tokens(s, h):
        other = soon if s == 1 else later[(s - 2) * tokens : (s - 1) * tokens]
        return jnp.concatenate([own[(s, h)], other[:, offsets[h] : offsets[h] + widths[h]]], axis=0)

    def gather(piece, h):
        pieces = [piece]
        for bit in ways[h][1]:
            pieces = pieces + [over_tensor(p, bit) for p in pieces]
        return pieces

    arrived = {(1, 0): gather(chip_tokens(1, 0), 0)}
    arrived[(1, 1)] = gather(chip_tokens(1, 1), 1)
    kv_partner = [over_tensor(x, way[0]) for x, way in zip((kv_out0, kv_out1), ways)]
    kv_partner_other = [over_core(x) for x in kv_partner]

    my_index = jnp.reshape(me, (1,)).astype(jnp.int32)

    def partner_part(s, h, behind):
        pieces = arrived[(s, h)]
        n = len(pieces)
        parts = [
            (i, c * tokens, n + c, i * tokens, tokens, None) for i in range(n) for c in range(2)
        ]
        return run_chunk(
            my_index, [*pieces, kv_partner[h], kv_partner_other[h]], parts, [], behind, "send"
        )

    def own_part(s, h, messages, behind, mode):
        pieces = arrived[(s, h)]
        n = len(pieces)
        parts = [
            (i, c * tokens, n + c, 0, tokens, ways[h][2][i]) for i in range(n) for c in range(2)
        ]
        return run_chunk(my_index, [*pieces, kv_grad, kv_other], parts, messages, behind, mode)

    keyed = [(4 * s + 2 * h, ("own", s, h)) for s in steps for h in range(2)]
    keyed += [(4 * s + 2 * h - 4 + (PARTNER_PLACE[h] + 0.1 * h if s > 1 else -3), ("partner", s, h)) for s in steps for h in range(2)]
    order = [kernel for _, kernel in sorted(keyed)]
    place = {kernel: i for i, kernel in enumerate(order)}
    released = {i: [] for i in range(len(order))}
    for s in steps[1:]:
        for h in range(2):
            released[max(place[("partner", s, h)] - GATHER_AHEAD[min(s, 3)][h], 0)].append((s, h))
    behind = arrived[(1, 1)][1:] + kv_partner_other[1:]
    from_partner, passed, grads, squares = {}, {}, [], []
    for i, (kind, s, h) in enumerate(order):
        if kind == "partner":
            out = partner_part(s, h, behind)
            from_partner[(s, h)] = over_tensor(out, ways[h][0])
        else:
            messages = [from_partner[(s, h)]] + ([passed[(h, s - 1)]] if s > 1 else [])
            if s < n_z:
                out = own_part(s, h, messages, behind, "send")
                passed[(h, s)] = hand_on(out, h)
            else:
                grad, out = own_part(s, h, messages, behind, "final")
                grads.append(grad)
                squares.append(out)
        behind = [out]
        if i == 0:
            later = over_core(after(later_out, out))
            kv_other = over_core(after(kv_grad, out))
        for then, half_then in released[i]:
            arrived[(then, half_then)] = gather(after(chip_tokens(then, half_then), out), half_then)

    square = squares[0] + squares[1]
    square = square + over_core(square)
    square = square + sum(over_tensor(square, m) for m in range(1, n_tensor))
    squares = [square] + [over_z(square, k) for k in range(1, n_z)]
    return tuple(adam_update(grads, squares, master, first, second, clip_limit))


def solution(mesh):
    in_specs = (
        P(("dp", "tensor"), None),
        P("dp", "tensor"),
        P("dp", "tensor"),
        P("dp", "tensor"),
        P("dp", "tensor"),
        P(),
    )
    out_specs = (P("dp", "tensor"), P("dp", "tensor"), P("dp", "tensor"))
    return jax.shard_map(
        functools.partial(on_device, mesh.shape["dp"], mesh.shape["tensor"]),
        mesh=mesh,
        in_specs=in_specs,
        out_specs=out_specs,
        check_vma=False,
    )
```

```python
import functools

import jax
import jax.numpy as jnp
from jax import lax
from jax.experimental import pallas as pl
from jax.experimental.pallas import tpu as pltpu
from jax.sharding import PartitionSpec as P

STEP = 20

beta_first = 0.9
beta_second = 0.95
learn_rate = 0.00015
decay_rate = 0.1

AXES = ("dp", "tensor")
SCALE_ROWS = 16
KNEE = 64.0
POWER = 32
SHIFT = 3.5
VMEM = 40 * 1024 * 1024

PARTNER_PLACE = (1, -1)
GATHER_AHEAD = {2: (2, 3), 3: (3, 3)}


def encode(values, scale):
    u = jnp.abs(values) * (KNEE / jnp.maximum(scale, 1e-30))
    w = (u + jnp.sqrt(u * u + 1.0)) * (2.0**-SHIFT)
    power = 1
    while power < POWER:
        w = w * w
        power *= 2
    return jnp.where(values < 0, -w, w).astype(jnp.bfloat16)


def decode(code, scale):
    code = code.astype(jnp.float32)
    log_w = jnp.log(jnp.maximum(jnp.abs(code), 2.0 ** (-SHIFT * POWER))) * (1.0 / POWER) + SHIFT * 0.6931471805599453
    u = jnp.exp(log_w) - jnp.exp(-log_w)
    size = u * (scale * (0.5 / KNEE))
    return jnp.where(code < 0, -size, size)


def tile_rows(rows):
    return 128 if rows % 128 == 0 else rows


def chunk_kernel(parts, n_arrays, n_in, mode, *refs):
    me = refs[0][0]
    array_refs, in_refs, rest = refs[1 : 1 + n_arrays], refs[1 + n_arrays : 1 + n_arrays + n_in], refs[1 + n_arrays + n_in :]
    (first_a, _, first_b, _, depth, _) = parts[0]
    rows, width = array_refs[first_a].shape[1], array_refs[first_b].shape[1]
    tile = tile_rows(rows)

    def values(at):
        total = None
        for a, a_row, b, b_row, depth, distance in parts:
            if distance is not None:
                b_row = pl.multiple_of((me ^ distance) * depth, 16)
            part = lax.dot_general(
                array_refs[a][pl.ds(a_row, depth), pl.ds(at, tile)],
                array_refs[b][pl.ds(b_row, depth), :],
                (((0,), (0,)), ((), ())),
                preferred_element_type=jnp.float32,
            )
            total = part if total is None else total + part
        for ref in in_refs:
            scale = ref[rows : rows + 1, :].astype(jnp.float32)
            total = total + decode(ref[pl.ds(at, tile), :], scale)
        return total

    if mode == "final":
        out_ref, square_ref = rest[-2:]
        square = jnp.zeros((8, width), jnp.float32)
        for at in range(0, rows, tile):
            total = values(at)
            out_ref[pl.ds(at, tile), :] = total
            square = square + jnp.sum((total * total).reshape(tile // 8, 8, width), axis=0)
        square_ref[...] = sum(square[:, s : s + 128] for s in range(0, width, 128))
        return
    out_ref, held = rest[-2:]
    largest = jnp.zeros((8, width), jnp.float32)
    for at in range(0, rows, tile):
        total = values(at)
        held[pl.ds(at, tile), :] = total
        largest = jnp.maximum(largest, jnp.max(jnp.abs(total).reshape(tile // 8, 8, width), axis=0))
    scale = jnp.max(largest, axis=0, keepdims=True).astype(jnp.bfloat16)
    out_ref[pl.ds(rows, SCALE_ROWS), :] = jnp.broadcast_to(scale, (SCALE_ROWS, width))
    scale = scale.astype(jnp.float32)
    for at in range(0, rows, tile):
        out_ref[pl.ds(at, tile), :] = encode(held[pl.ds(at, tile), :], scale)


def run_chunk(me, arrays, parts, messages, after, mode):
    rows, width = arrays[parts[0][0]].shape[1], arrays[parts[0][2]].shape[1]
    if mode == "final":
        out_shape = (
            jax.ShapeDtypeStruct((rows, width), jnp.float32),
            jax.ShapeDtypeStruct((8, 128), jnp.float32),
        )
        scratch = []
    else:
        out_shape = jax.ShapeDtypeStruct((rows + SCALE_ROWS, width), jnp.bfloat16)
        scratch = [pltpu.VMEM((rows, width), jnp.float32)]
    cost = pl.CostEstimate(flops=1024, bytes_accessed=1024, transcendentals=0)
    whole = pl.BlockSpec(memory_space=pltpu.VMEM)
    return pl.pallas_call(
        functools.partial(chunk_kernel, parts, len(arrays), len(messages), mode),
        out_shape=out_shape,
        in_specs=[pl.BlockSpec(memory_space=pltpu.SMEM)]
        + [whole] * (len(arrays) + len(messages))
        + [pl.BlockSpec(memory_space=pl.ANY)] * len(after),
        scratch_shapes=scratch,
        cost_estimate=cost,
        compiler_params=pltpu.CompilerParams(vmem_limit_bytes=VMEM),
    )(me, *arrays, *messages, *after)


def pack_kernel(copies, where, inputs, kv_grad, behind, *outs):
    for source, index, out, row, rows, column, columns in copies:
        to = outs[out].at[pl.ds(row, rows), pl.ds(column, columns)]
        if source == "columns":
            to[...] = inputs[:, pl.ds(pl.multiple_of(where[index], 128), columns)]
        else:
            to[...] = kv_grad[pl.ds(pl.multiple_of(where[index], 16), rows), :]


def pack(where, inputs, kv_grad, copies, shapes, behind):
    whole = pl.BlockSpec(memory_space=pltpu.VMEM)
    return pl.pallas_call(
        functools.partial(pack_kernel, copies),
        out_shape=[jax.ShapeDtypeStruct(shape, jnp.bfloat16) for shape in shapes],
        in_specs=[pl.BlockSpec(memory_space=pltpu.SMEM), whole, whole, pl.BlockSpec(memory_space=pl.ANY)],
        out_specs=[whole] * len(shapes),
        cost_estimate=pl.CostEstimate(flops=1024, bytes_accessed=1024, transcendentals=0),
        compiler_params=pltpu.CompilerParams(vmem_limit_bytes=VMEM),
    )(where, inputs, kv_grad, behind)


def adam_kernel(n_grads, n_squares, *refs):
    clip_limit = refs[0]
    grads = refs[1 : 1 + n_grads]
    squares = refs[1 + n_grads : 1 + n_grads + n_squares]
    state = refs[1 + n_grads + n_squares :][:3]
    outs = refs[4 + n_grads + n_squares :][:3]
    held, sems = refs[-2:]
    square_sum = squares[0][...]
    for square in squares[1:]:
        square_sum = square_sum + square[...]
    grad_norm = jnp.sqrt(jnp.sum(square_sum, keepdims=True))
    clip_factor = jnp.minimum(1.0, clip_limit[0] / (grad_norm + 1e-06))
    start = 0
    copies = []
    for grad in grads:
        tile = tile_rows(grad.shape[0]) // 2
        for at in range(0, grad.shape[0], tile):
            here = pl.ds(start, tile)
            master, first, second = [ref[here, :] for ref in state]
            scaled = grad[pl.ds(at, tile), :] * clip_factor
            new_first = beta_first * first + (1.0 - beta_first) * scaled
            new_second = beta_second * second + (1.0 - beta_second) * scaled * scaled
            first_hat = new_first * (1.0 / (1.0 - beta_first**STEP))
            second_hat = new_second * (1.0 / (1.0 - beta_second**STEP))
            new_master = master - learn_rate * (
                first_hat / (second_hat * lax.rsqrt(second_hat) + 1e-08) + decay_rate * master
            )
            for i, value in enumerate((new_master, new_first, new_second)):
                held[i, here, :] = value
                copy = pltpu.make_async_copy(held.at[i, here, :], outs[i].at[here, :], sems.at[len(copies)])
                copy.start()
                copies.append(copy)
            start += tile
    for copy in copies:
        copy.wait()


def adam_update(grads, squares, master, first, second, clip_limit):
    whole = pl.BlockSpec(memory_space=pltpu.VMEM)
    n_copies = 6 * sum(grad.shape[0] // tile_rows(grad.shape[0]) for grad in grads)
    return pl.pallas_call(
        functools.partial(adam_kernel, len(grads), len(squares)),
        out_shape=[jax.ShapeDtypeStruct(master.shape, jnp.float32)] * 3,
        in_specs=[pl.BlockSpec(memory_space=pltpu.SMEM)] + [whole] * (len(grads) + len(squares) + 3),
        out_specs=[pl.BlockSpec(memory_space=pl.ANY)] * 3,
        scratch_shapes=[
            pltpu.VMEM((3, *master.shape), jnp.float32),
            pltpu.SemaphoreType.DMA((n_copies,)),
        ],
        cost_estimate=pl.CostEstimate(flops=1024, bytes_accessed=1024, transcendentals=0),
        compiler_params=pltpu.CompilerParams(vmem_limit_bytes=VMEM),
    )(clip_limit, *grads, *squares, master, first, second)


def on_device(n_dp, n_tensor, inputs, kv_grad, master, first, second, clip_limit):
    n_z = n_dp // 2
    dp, me = lax.axis_index("dp"), lax.axis_index("tensor")
    z, core = dp // 2, dp % 2
    tokens, block = inputs.shape[0], master.shape[0]
    widths = [block // 2] * 2
    offsets = [0, block // 2]

    def send(x, move):
        pairs = []
        for g in range(n_dp):
            for t in range(n_tensor):
                to = move(g // 2, g % 2, t)
                if to is not None:
                    pairs.append((g * n_tensor + t, (to[0] * 2 + to[1]) * n_tensor + to[2]))
        return lax.ppermute(x, AXES, pairs)

    def over_core(x):
        return send(x, lambda z, c, t: (z, 1 - c, t))

    def over_tensor(x, bit):
        return send(x, lambda z, c, t: (z, c, t ^ bit))

    def over_z(x, bits):
        return send(x, lambda z, c, t: (z ^ bits, c, t))

    def place_of(z):
        return jnp.where(z % 2 == 0, z // 2, n_z - (z + 1) // 2)

    def at_place(place):
        place = place % n_z
        return jnp.where(place < (n_z + 1) // 2, 2 * place, 2 * (n_z - place) - 1)

    ring = list(range(0, n_z, 2)) + list(range(n_z - 1 - n_z % 2, 0, -2))
    ways_round = (1, -1)

    def hand_on(x, h):
        return send(x, lambda z, c, t: (ring[(ring.index(z) + ways_round[h]) % n_z], c, t))

    def columns(s, owner_core, h):
        owner = at_place(place_of(z) - ways_round[h] * s)
        return (owner * 2 + owner_core) * block + offsets[h]

    steps = list(range(1, n_z + 1))

    def after(x, *others):
        return lax.optimization_barrier((x, *others))[0]

    bits = [1 << i for i in range((n_tensor - 1).bit_length())]
    ways = []
    for q in range(2):
        partner = bits[q]
        gather = [bit for bit in bits if bit != partner]
        at = [0]
        for bit in gather:
            at = at + [m ^ bit for m in at]
        ways.append((partner, gather, at))

    pieces = [(s, h) for s in steps for h in range(2)]
    where = [columns(s, core, h) for s, h in pieces] + [columns(s, 1 - core, h) for s, h in pieces]
    where += [(me ^ partner ^ m) * tokens for partner, _, at in ways for m in at]
    where = jnp.stack(where).astype(jnp.int32)
    n, n_at = len(pieces), len(ways[0][2])
    copies = [
        ("rows", 2 * n + q * n_at + i, q, i * tokens, tokens, 0, kv_grad.shape[1])
        for q in range(2)
        for i in range(n_at)
    ]
    kv_out0, kv_out1 = pack(where, kv_grad, kv_grad, copies, [(n_at * tokens, kv_grad.shape[1])] * 2, where)
    shapes = [(tokens, block)] + [(tokens, width) for width in widths]
    copies = [("columns", n + h, 0, 0, tokens, offsets[h], widths[h]) for h in range(2)]
    copies += [("columns", h, 1 + h, 0, tokens, 0, widths[h]) for h in range(2)]
    soon_out, *own = pack(where, inputs, kv_grad, copies, shapes, kv_out0)
    shapes = [((n_z - 1) * tokens, block)] + [(tokens, widths[h]) for _, h in pieces[2:]]
    copies = [
        ("columns", n + i, 0, (s - 2) * tokens, tokens, offsets[h], widths[h])
        for i, (s, h) in enumerate(pieces)
        if s > 1
    ]
    copies += [("columns", i, i - 1, 0, tokens, 0, widths[h]) for i, (s, h) in enumerate(pieces) if s > 1]
    later_out, *own_then = pack(where, inputs, kv_grad, copies, shapes, soon_out)
    own = dict(zip(pieces, own + own_then))

    soon = over_core(soon_out)
    def chip_tokens(s, h):
        other = soon if s == 1 else later[(s - 2) * tokens : (s - 1) * tokens]
        return jnp.concatenate([own[(s, h)], other[:, offsets[h] : offsets[h] + widths[h]]], axis=0)

    def gather(piece, h):
        pieces = [piece]
        for bit in ways[h][1]:
            pieces = pieces + [over_tensor(p, bit) for p in pieces]
        return pieces

    arrived = {(1, 0): gather(chip_tokens(1, 0), 0)}
    arrived[(1, 1)] = gather(chip_tokens(1, 1), 1)
    kv_partner = [over_tensor(x, way[0]) for x, way in zip((kv_out0, kv_out1), ways)]
    kv_partner_other = [over_core(x) for x in kv_partner]

    my_index = jnp.reshape(me, (1,)).astype(jnp.int32)

    def partner_part(s, h, behind):
        pieces = arrived[(s, h)]
        n = len(pieces)
        parts = [
            (i, c * tokens, n + c, i * tokens, tokens, None) for i in range(n) for c in range(2)
        ]
        return run_chunk(
            my_index, [*pieces, kv_partner[h], kv_partner_other[h]], parts, [], behind, "send"
        )

    def own_part(s, h, messages, behind, mode):
        pieces = arrived[(s, h)]
        n = len(pieces)
        parts = [
            (i, c * tokens, n + c, 0, tokens, ways[h][2][i]) for i in range(n) for c in range(2)
        ]
        return run_chunk(my_index, [*pieces, kv_grad, kv_other], parts, messages, behind, mode)

    keyed = [(4 * s + 2 * h, ("own", s, h)) for s in steps for h in range(2)]
    keyed += [(4 * s + 2 * h - 4 + (PARTNER_PLACE[h] + 0.1 * h if s > 1 else -3), ("partner", s, h)) for s in steps for h in range(2)]
    order = [kernel for _, kernel in sorted(keyed)]
    place = {kernel: i for i, kernel in enumerate(order)}
    released = {i: [] for i in range(len(order))}
    for s in steps[1:]:
        for h in range(2):
            released[max(place[("partner", s, h)] - GATHER_AHEAD[min(s, 3)][h], 0)].append((s, h))
    behind = arrived[(1, 1)][1:] + kv_partner_other[1:]
    from_partner, passed, grads, squares = {}, {}, [], []
    for i, (kind, s, h) in enumerate(order):
        if kind == "partner":
            out = partner_part(s, h, behind)
            from_partner[(s, h)] = over_tensor(out, ways[h][0])
        else:
            messages = [from_partner[(s, h)]] + ([passed[(h, s - 1)]] if s > 1 else [])
            if s < n_z:
                out = own_part(s, h, messages, behind, "send")
                passed[(h, s)] = hand_on(out, h)
            else:
                grad, out = own_part(s, h, messages, behind, "final")
                grads.append(grad)
                squares.append(out)
        behind = [out]
        if i == 0:
            later = over_core(after(later_out, out))
            kv_other = over_core(after(kv_grad, out))
        for then, half_then in released[i]:
            arrived[(then, half_then)] = gather(after(chip_tokens(then, half_then), out), half_then)

    square = squares[0] + squares[1]
    square = square + over_core(square)
    steps_z = [1 << i for i in range((n_z - 1).bit_length())]
    for bit in steps_z:
        square = square + over_z(square, bit)
    for bit in bits[:-1]:
        square = square + over_tensor(square, bit)
    squares = [square, over_tensor(square, bits[-1])]
    return tuple(adam_update(grads, squares, master, first, second, clip_limit))


def solution(mesh):
    in_specs = (
        P(("dp", "tensor"), None),
        P("dp", "tensor"),
        P("dp", "tensor"),
        P("dp", "tensor"),
        P("dp", "tensor"),
        P(),
    )
    out_specs = (P("dp", "tensor"), P("dp", "tensor"), P("dp", "tensor"))
    return jax.shard_map(
        functools.partial(on_device, mesh.shape["dp"], mesh.shape["tensor"]),
        mesh=mesh,
        in_specs=in_specs,
        out_specs=out_specs,
        check_vma=False,
    )
```
